32 devices in a mesh: groups: 2 (over x), docs: 16 (over z, y, core).
Axes of the slice: x: 2, y: 2, z: 4, core: 2. Of those that a mesh axis runs over, the one named last changes fastest.
Arguments:
- query_act: bfloat16 [8, 16, 8192], P('groups'), parts along dimension 0, may hold values from -6 to 6
- query_grad: bfloat16 [8, 16, 7168], P('groups', None, 'docs'), parts along dimension 0, may hold values from -6 to 6
- eigenvalues: bfloat16 [8192, 7168], P(None, 'docs'), may hold values from 0.049804688 to 1
- doc_act: bfloat16 [32, 6, 8192], P(('groups', 'docs')), parts along dimension 0, may hold values from -6 to 6
- doc_grad: bfloat16 [32, 6, 7168], P(('groups', 'docs')), parts along dimension 0, may hold values from -6 to 6
- doc_len: int32 [32], P(('groups', 'docs')), parts along dimension 0, may hold values from 1 to 6, 56 in all
Outputs:
- scores: float32 [4, 32], P(None, ('groups', 'docs')), parts along dimension 1
The draws below stay inside these ranges and needn't reach their ends.
There are 2 independent parts, one for each index of `groups`. The reference program is written for one: setup_inputs(seed, part) draws one part's arguments, and reference() takes and returns one part's arrays. A program takes and returns all parts, laid end to end along the dimension named above; an argument that names none is the same for every part. Nothing has to cross between parts.
Inputs may be any that keep to these rules, and one draw needn't show every extreme that they name: `doc_len`: token counts of the documents; at least one document has all 6 slots live.
All inputs are finite; a program needn't handle non-finite values. No bound on the sum of `doc_len` on one device may be relied on, other than what follows from the above.
Results may differ from the reference program's by a relative error of at most 0.0035.
Values may be sent and summed in bfloat16 or wider, within the bound.
A program may use at most 192 MiB of HBM per device.

```python
import math
import jax
import jax.numpy as jnp
import numpy as np
from jax import lax

D = 8192
FF_DEV = 448
QRY = 4
QTOK = 16
DOC_TOK = 6
FF = 7168
DOCS = 16
N_DOCS = 16


def strengthened(entries, stream_key, source, target, blocks, factor):
    owner, partner = [(jnp.arange(entries.shape[position]) // (entries.shape[position] // blocks)).reshape([-1 if axis == position else 1 for axis in range(entries.ndim)]) for position in (source, target)]
    chosen = jax.random.permutation(stream_key, blocks)[partner]
    strong = (owner == chosen) | (owner == (partner + blocks // 2) % blocks)
    return jnp.where(strong, factor * entries, entries)


def level_of(stream_key, extent, cuts, least, top_value):
    loudness = 1.0
    for axis_at, blocks in cuts:
        heights = jax.random.uniform(jax.random.fold_in(jax.random.fold_in(stream_key, 6), axis_at), (blocks,), jnp.float32, least / len(cuts), top_value / len(cuts))
        loudness = loudness * jnp.repeat(jnp.exp(heights), extent[axis_at] // blocks).reshape((-1,) + (1,) * (len(extent) - 1 - axis_at))
    return loudness


def split_up(count, total, limit, slope):
    loads = [(1 << 20) // math.isqrt(rank ** slope) + 1 for rank in range(2, count + 1)]
    rest, holding = total - limit - (count - 1), [1] * (count - 1)
    while rest > 0:
        candidates = [i for i in range(count - 1) if holding[i] < limit]
        mass, remaining = sum([loads[i] for i in candidates]), rest
        for i in candidates:
            extra = min(limit - holding[i], max(1, remaining * loads[i] // mass), rest)
            holding[i] = holding[i] + extra
            rest = rest - extra
    return np.array([limit] + holding)


def ragged(own_key, number_of, total, most, slope):
    if number_of == 2:
        one = jax.random.randint(own_key, (), max(1, total - most), min(most, total - 1) + 1)
        return jnp.stack([one, total - one])
    sizes = jnp.asarray(split_up(number_of, total, most, slope), jnp.int32)
    pairs = (number_of - 1) // 2
    source_of, taker = sizes[1:1 + 2 * pairs:2], sizes[2:2 + 2 * pairs:2]
    room = jnp.minimum(source_of - 1, most - taker)
    moved = jax.random.randint(jax.random.fold_in(own_key, 1), (pairs,), 0, 1 << 20) % (room + 1)
    sizes = sizes.at[1:1 + 2 * pairs:2].set(source_of - moved).at[2:2 + 2 * pairs:2].set(taker + moved)
    return sizes[jax.random.permutation(jax.random.fold_in(own_key, 2), number_of)]


def bell_draw(key, extent, scale, reach, shards=(), kind=jnp.bfloat16):
    array = jax.random.normal(key, extent, jnp.float32) * scale
    if len(shards) > 0:
        array = level_of(key, extent, shards, -0.22, 0.18) * array
    return jnp.clip(array, min=-reach, max=reach).astype(kind)


def noise_with(key, dims, deviation, most, pieces, heavy, kind=jnp.bfloat16):
    entries = deviation * jax.random.normal(key, dims, jnp.float32)
    if pieces:
        entries = entries * level_of(key, dims, pieces, -0.22, 0.18)
    return jnp.clip(strengthened(entries, jax.random.fold_in(key, 3), *heavy), -most, most).astype(kind)


def setup_inputs(seed: int = 0, part: int = 0) -> dict:
    splits = jax.random.split(jax.random.key(seed), 7)
    part_splits = jax.random.split(jax.random.fold_in(splits[6], part), 7)
    return {
        "query_act": bell_draw(part_splits[0], (QRY, QTOK, D), 1.0, 6.0),
        "query_grad": bell_draw(part_splits[1], (QRY, QTOK, FF), 1.0, 6.0, ((2, 16),)),
        "eigenvalues": jnp.clip(jnp.exp(math.log(1.0) - 2.9996462 * jax.random.uniform(splits[2], (D, FF), jnp.float32) ** level_of(splits[2], (D, FF), ((1, 16),), -0.2, 0.2)), 0.049804688, 1.0).astype(jnp.bfloat16),
        "doc_act": bell_draw(part_splits[3], (DOCS, DOC_TOK, D), 1.0, 6.0, ((0, 16),)),
        "doc_grad": noise_with(part_splits[4], (DOCS, DOC_TOK, FF), 1.0, 6.0, ((0, 16),), (2, 0, 16, 2.0)),
        "doc_len": ragged(part_splits[5], DOCS, DOCS * (DOC_TOK + 1) // 2, DOC_TOK, 0).astype(jnp.int32),
    }


damping = 0.05

def reference(query_act, query_grad, eigenvalues, doc_act, doc_grad, doc_len):
    positions = jnp.arange(DOC_TOK, dtype=jnp.int32)
    alive_mask = positions[None, :] < doc_len.astype(jnp.int32)[:, None]
    masked = jnp.where(alive_mask[:, :, None], doc_grad, jnp.zeros((), doc_grad.dtype))
    act_rows = doc_act.reshape(DOCS * DOC_TOK, D)
    grad_blocks = masked.reshape(DOCS * DOC_TOK, N_DOCS, FF_DEV).transpose(1, 0, 2)
    eig_blocks = eigenvalues.reshape(D, N_DOCS, FF_DEV).transpose(1, 0, 2)
    qgrad_blocks = query_grad.reshape(QRY, QTOK, N_DOCS, FF_DEV).transpose(2, 0, 1, 3)

    def one_block(operands):
        eig_slab, qgrad_slab, dgrad_slab = operands
        damped = eig_slab.astype(jnp.float32) + damping
        columns = []
        for query in range(QRY):
            gram = lax.dot_general(query_act[query], qgrad_slab[query], (((0,), (0,)), ((), ())), preferred_element_type=jnp.float32)
            precond = (gram / damped).astype(jnp.bfloat16)
            image = jnp.dot(act_rows, precond, preferred_element_type=jnp.float32)
            weighted = lax.optimization_barrier(jnp.sum(image * dgrad_slab.astype(jnp.float32), axis=1))
            columns.append(lax.optimization_barrier(jnp.sum(weighted.reshape(DOCS, DOC_TOK), axis=1)))
        return jnp.stack(columns)
    partials = lax.map(one_block, (eig_blocks, qgrad_blocks, grad_blocks))
    norm_factor = 1.0 / (5.0 * math.sqrt(QTOK * D * FF * DOC_TOK))
    return lax.optimization_barrier(jnp.sum(partials, axis=0)) * norm_factor
```

```python
import functools
import math

import jax
import jax.numpy as jnp
from jax import lax
from jax.experimental import pallas as pl
from jax.experimental.pallas import tpu as pltpu
from jax.sharding import PartitionSpec as P

damping = 0.05
MESH = pl.DeviceIdType.MESH
f32 = jnp.float32
bf16 = jnp.bfloat16

FOLDS = 8
CHUNK = 256
EIG_SLOTS = 4


def kernel(n, scale, len_ref, qact_ref, qgrad_ref, eig_ref, dact_ref, dgrad_ref, out_ref,
           buf, wide, actb, pre, eigv, qt, bd, own, gown, gtmp, gsend, grecv, gwide, acc, part, parts,
           eig_sem, ring_send, ring_recv, cross_send, cross_recv, g_send, g_recv, p_send, p_recv):
    queries, qtokens, width = qact_ref.shape
    tokens = dact_ref.shape[1]
    slab = eig_ref.shape[1]
    fold = width // FOLDS
    half = fold // 2
    full = slab // 128
    chips = n // 2
    hops = chips // 2
    groups = chips
    group_rows = width // groups
    me = lax.axis_index("docs")
    core = lax.rem(me, 2)
    chip = me // 2
    snake = n == 16

    if snake:
        pos = chip // 2 + lax.rem(chip, 2) * (chips - 1 - 2 * (chip // 2))
    else:
        pos = chip

    def device_at(p, c):
        p = lax.rem(p + 2 * chips, chips)
        if snake:
            y = p // hops
            return 2 * (2 * (p + y * (chips - 1 - 2 * p)) + y) + c
        return 2 * p + c

    def eig_copy(g):
        slot = lax.rem(g, EIG_SLOTS)
        return pltpu.make_async_copy(
            eig_ref.at[pl.ds(pl.multiple_of(g * group_rows, group_rows), group_rows)],
            eigv.at[slot], eig_sem.at[slot])

    for g in range(EIG_SLOTS - 1):
        eig_copy(g).start()

    barrier = pltpu.get_barrier_semaphore()

    @pl.loop(1, n)
    def _(r):
        pl.semaphore_signal(barrier, inc=1, device_id={"docs": lax.rem(me + r, n)}, device_id_type=MESH)

    mine = dact_ref[0].astype(f32)
    for k in range(FOLDS):
        for b in range(fold // 128):
            at = k * fold + b * 128
            own[b, pl.ds(k, tokens, stride=FOLDS), :] = mine[:, at:at + 128]
    for b in range(fold // 128):
        buf[me, :, b * 128:(b + 1) * 128] = own[b].astype(bf16)

    def ring_copy(way, step, h):
        sign = 1 - 2 * way
        block = device_at(pos - sign * (step - 1), core)
        view = buf.at[block, :, pl.ds(pl.multiple_of(h * half, half), half)]
        return pltpu.make_async_remote_copy(
            src_ref=view, dst_ref=view,
            send_sem=ring_send.at[way, step - 1, h], recv_sem=ring_recv.at[way, step - 1, h],
            device_id={"docs": device_at(pos + sign, core)}, device_id_type=MESH)

    def ring_arrival(way, step, h):
        sign = 1 - 2 * way
        block = device_at(pos - sign * step, core)
        view = buf.at[block, :, pl.ds(pl.multiple_of(h * half, half), half)]
        return pltpu.make_async_remote_copy(
            src_ref=view, dst_ref=view,
            send_sem=ring_send.at[way, step - 1, h], recv_sem=ring_recv.at[way, step - 1, h],
            device_id={"docs": device_at(pos + sign, core)}, device_id_type=MESH)

    def cross_copy(p, c):
        p = lax.rem(p + 2 * chips, chips)
        view = buf.at[device_at(p, c)]
        return pltpu.make_async_remote_copy(
            src_ref=view, dst_ref=view,
            send_sem=cross_send.at[p], recv_sem=cross_recv.at[p],
            device_id={"docs": 2 * chip + 1 - core}, device_id_type=MESH)

    pl.semaphore_wait(barrier, n - 1)
    for h in range(2):
        for way in range(2):
            ring_copy(way, 1, h).start()
    cross_copy(pos, core).start()

    bd[...] = jnp.zeros_like(bd)
    for q in range(queries):
        rows = slice(q * qtokens, (q + 1) * qtokens)
        for j in range(full):
            at = (j * queries + q) * 128
            bd[rows, at:at + 128] = qgrad_ref[q, :, j * 128:(j + 1) * 128]
        rest = qgrad_ref[q, :, full * 128:]
        none = jnp.zeros_like(rest)
        at = (full * queries + q // 2) * 128
        bd[rows, at:at + 128] = jnp.concatenate([rest, none] if q % 2 == 0 else [none, rest], axis=1)
    for q in range(queries):
        rows = slice(q * qtokens, (q + 1) * qtokens)
        qt[rows, :] = qact_ref[q]

    def make_pre(g):
        slot = lax.rem(g, EIG_SLOTS)
        eig_copy(g).wait()

        @pl.when(g + EIG_SLOTS - 1 < groups)
        def _():
            eig_copy(g + EIG_SLOTS - 1).start()

        @pl.loop(0, group_rows // CHUNK)
        def _(c):
            local = pl.multiple_of(c * CHUNK, CHUNK)
            at = pl.multiple_of(g * group_rows + c * CHUNK, CHUNK)
            left = qt[:, pl.ds(at, CHUNK)].T
            inv = 1.0 / (eigv[slot, pl.ds(local, CHUNK), :].astype(f32) + damping)
            tail = inv[:, full * 128:]
            tail = jnp.concatenate([tail, tail], axis=1)
            for pair in range(bd.shape[1] // 256):
                cols = slice(pair * 256, pair * 256 + 256)
                gram = jnp.dot(left, bd[:, cols], preferred_element_type=f32)
                for side in range(2):
                    j = (pair * 2 + side) // queries
                    w = inv[:, j * 128:(j + 1) * 128] if j < full else tail
                    lo = pair * 256 + side * 128
                    pre[pl.ds(at, CHUNK), lo:lo + 128] = (gram[:, side * 128:side * 128 + 128] * w).astype(bf16)

    @pl.loop(0, chips - 2)
    def _(e):
        make_pre(e)
        step = e // 2 + 1
        h = lax.rem(e, 2)
        for way in range(2):
            ring_arrival(way, step, h).wait_recv()

            @pl.when(step + 1 < hops)
            def _():
                ring_copy(way, step + 1, h).start()

        @pl.when(e == chips - 4)
        def _():
            ring_copy(0, hops, 0).start()

        @pl.when(e == chips - 3)
        def _():
            ring_copy(1, hops, 1).start()

        @pl.when(h == 1)
        def _():
            cross_copy(pos - step, core).start()
            cross_copy(pos + step, core).start()

    slot_of = lax.broadcasted_iota(jnp.int32, (tokens, dgrad_ref.shape[2]), 0)
    gown[...] = jnp.where(slot_of < len_ref[0], dgrad_ref[0].astype(f32), 0.0)
    gtmp[...] = jnp.zeros_like(gtmp)

    def g_copy(slot, to):
        return pltpu.make_async_remote_copy(
            src_ref=gsend.at[to], dst_ref=grecv.at[slot],
            send_sem=g_send.at[to], recv_sem=g_recv.at[slot],
            device_id={"docs": to}, device_id_type=MESH)

    @pl.loop(0, n)
    def _(r):
        to = lax.rem(me + r, n)
        start = pl.multiple_of((to * slab) // 128 * 128, 128)
        for side in range(2):
            for b in range(2):
                at = pl.multiple_of(start + side * 256 + b * 128, 128)
                gtmp[b, pl.ds(side, tokens, stride=2), :] = gown[:, pl.ds(at, 128)]
        cut = jnp.concatenate([gtmp[0], gtmp[1]], axis=1).astype(bf16)
        gsend[to] = cut

        @pl.when(r == 0)
        def _():
            grecv[me] = cut

        @pl.when(r > 0)
        def _():
            g_copy(me, to).start()

    make_pre(chips - 2)
    ring_arrival(0, hops, 0).wait_recv()
    ring_arrival(1, hops, 1).wait_recv()
    cross_copy(pos + hops, core).start()
    make_pre(chips - 1)

    @pl.loop(0, chips)
    def _(p):
        cross_copy(p, 1 - core).wait_recv()

    @pl.loop(0, n)
    def _(d):
        block = buf[d].astype(f32)
        for t in range(tokens):
            at = pl.ds(pl.multiple_of((t * n + d) * FOLDS, FOLDS), FOLDS)
            for b in range(fold // 128):
                wide[b, at, :] = block[t * FOLDS:(t + 1) * FOLDS, b * 128:(b + 1) * 128]


    acc[...] = jnp.zeros_like(acc)

    @pl.loop(0, FOLDS)
    def _(k):
        rows = pl.ds(pl.multiple_of(k * fold, fold), fold)
        for b in range(fold // 128):
            actb[:, b * 128:(b + 1) * 128] = wide[b, pl.ds(k, tokens * n, stride=FOLDS), :].astype(bf16)
        for pair in range(bd.shape[1] // 256):
            cols = slice(pair * 256, pair * 256 + 256)
            acc[:, cols] += jnp.dot(actb[...], pre[rows, cols], preferred_element_type=f32)

    @pl.loop(1, n)
    def _(r):
        g_copy(lax.rem(me + r, n), me).wait_recv()

    @pl.loop(0, n)
    def _(d):
        got = grecv[d].astype(f32)
        for b in range(2):
            gwide[b, pl.ds(pl.multiple_of(d * 16, 16), 16), :] = got[:, b * 128:(b + 1) * 128]

    part[...] = jnp.zeros_like(part)
    odd = lax.rem(me, 2) == 1
    sums = [jnp.zeros((n, 128), f32) for _ in range(queries)]
    low = lax.broadcasted_iota(jnp.int32, (n, 128), 1) < slab - full * 128
    for t in range(tokens):
        window = jnp.concatenate(
            [gwide[b, pl.ds(t * 2 + side, n, stride=16), :] for side in range(2) for b in range(2)], axis=1)
        moved = jnp.concatenate([window[:, 64:], window[:, :64]], axis=1)
        grad = jnp.where(odd, moved, window)
        last = grad[:, full * 128:full * 128 + 64]
        last = jnp.concatenate([last, last], axis=1)
        rows = slice(t * n, (t + 1) * n)
        for q in range(queries):
            for j in range(full):
                at = (j * queries + q) * 128
                sums[q] += acc[rows, at:at + 128] * grad[:, j * 128:(j + 1) * 128]
            at = (full * queries + q // 2) * 128
            both = acc[rows, at:at + 128] * last
            sums[q] += jnp.where(low if q % 2 == 0 else jnp.logical_not(low), both, 0.0)
    for q in range(queries):
        part[pl.ds(q, n, stride=8), :] = sums[q]

    def p_copy(slot, to):
        return pltpu.make_async_remote_copy(
            src_ref=part.at[pl.ds(pl.multiple_of(to * 8, 8), 8)],
            dst_ref=parts.at[pl.ds(pl.multiple_of(slot * 8, 8), 8)],
            send_sem=p_send.at[to], recv_sem=p_recv.at[slot],
            device_id={"docs": to}, device_id_type=MESH)

    @pl.loop(1, n)
    def _(r):
        p_copy(me, lax.rem(me + r, n)).start()

    mine_at = pl.ds(pl.multiple_of(me * 8, 8), 8)
    parts[mine_at, :] = part[mine_at, :]

    for h in range(2):
        for way in range(2):
            @pl.loop(1, hops)
            def _(s):
                ring_copy(way, s, h).wait_send()
    ring_copy(0, hops, 0).wait_send()
    ring_copy(1, hops, 1).wait_send()

    @pl.loop(0, chips)
    def _(p):
        cross_copy(p, core).wait_send()

    @pl.loop(1, n)
    def _(r):
        g_copy(me, lax.rem(me + r, n)).wait_send()

    @pl.loop(1, n)
    def _(r):
        p_copy(lax.rem(me + r, n), me).wait_recv()

    total = parts[0:8, :]
    for d in range(1, n):
        total += parts[d * 8:d * 8 + 8, :]
    out_ref[...] = jnp.sum(total, axis=1, keepdims=True)[:queries] * scale

    @pl.loop(1, n)
    def _(r):
        p_copy(me, lax.rem(me + r, n)).wait_send()


def body(query_act, query_grad, eigenvalues, doc_act, doc_grad, doc_len):
    queries, qtokens, width = query_act.shape
    tokens = doc_act.shape[1]
    slab = eigenvalues.shape[1]
    n = lax.axis_size("docs")
    chips = n // 2
    fold = width // FOLDS
    columns = queries * slab
    scale = 1.0 / (5.0 * math.sqrt(qtokens * width * slab * n * tokens))
    vmem = pl.BlockSpec(memory_space=pltpu.VMEM)
    dma = pltpu.SemaphoreType.DMA
    return pl.pallas_call(
        functools.partial(kernel, n, scale),
        out_shape=jax.ShapeDtypeStruct((queries, 1), f32),
        in_specs=[pl.BlockSpec(memory_space=pltpu.SMEM), vmem, vmem, pl.BlockSpec(memory_space=pl.ANY), vmem, vmem],
        out_specs=vmem,
        scratch_shapes=[
            pltpu.VMEM((n, tokens * FOLDS, fold), bf16),
            pltpu.VMEM((fold // 128, n * tokens * FOLDS, 128), f32),
            pltpu.VMEM((n * tokens, fold), bf16),
            pltpu.VMEM((width, columns), bf16),
            pltpu.VMEM((EIG_SLOTS, width // chips, slab), bf16),
            pltpu.VMEM((queries * qtokens, width), bf16),
            pltpu.VMEM((queries * qtokens, columns), bf16),
            pltpu.VMEM((fold // 128, tokens * FOLDS, 128), f32),
            pltpu.VMEM((tokens, doc_grad.shape[2]), f32),
            pltpu.VMEM((2, 16, 128), f32),
            pltpu.VMEM((n, 16, 256), bf16),
            pltpu.VMEM((n, 16, 256), bf16),
            pltpu.VMEM((2, n * 16, 128), f32),
            pltpu.VMEM((n * tokens, columns), f32),
            pltpu.VMEM((n * 8, 128), f32),
            pltpu.VMEM((n * 8, 128), f32),
            dma((EIG_SLOTS,)),
            dma((2, chips // 2, 2)),
            dma((2, chips // 2, 2)),
            dma((chips,)),
            dma((chips,)),
            dma((n,)),
            dma((n,)),
            dma((n,)),
            dma((n,)),
        ],
        compiler_params=pltpu.CompilerParams(
            collective_id=0, has_side_effects=True, vmem_limit_bytes=62 * 1024 * 1024),
    )(doc_len, query_act, query_grad, eigenvalues, doc_act, doc_grad)


def solution(mesh):
    in_specs = (
        P("groups", None, None),
        P("groups", None, "docs"),
        P(None, "docs"),
        P(("groups", "docs"), None, None),
        P(("groups", "docs"), None, None),
        P(("groups", "docs")),
    )
    out_specs = P(None, ("groups", "docs"))
    return jax.shard_map(body, mesh=mesh, in_specs=in_specs, out_specs=out_specs, check_vma=False)
```

```python
import functools
import math

import jax
import jax.numpy as jnp
from jax import lax
from jax.experimental import pallas as pl
from jax.experimental.pallas import tpu as pltpu
from jax.sharding import PartitionSpec as P

damping = 0.05
MESH = pl.DeviceIdType.MESH
f32 = jnp.float32
bf16 = jnp.bfloat16

FOLDS = 8
CHUNK = 256
EIG_SLOTS = 4


def kernel(n, scale, len_ref, qact_ref, qgrad_ref, eig_ref, dact_ref, dgrad_ref, out_ref,
           buf, wide, actb, pre, eigv, qgt, own, gown, gtmp, gsend, grecv, gwide, grads, gradt, acc, rows, part, parts,
           eig_sem, ring_send, ring_recv, cross_send, cross_recv, g_send, g_recv, p_send, p_recv):
    queries, qtokens, width = qact_ref.shape
    tokens = dact_ref.shape[1]
    slab = eig_ref.shape[0]
    fold = width // FOLDS
    half = fold // 2
    chips = n // 2
    hops = chips // 2
    groups = chips
    group_rows = width // groups
    me = lax.axis_index("docs")
    core = lax.rem(me, 2)
    chip = me // 2
    snake = n == 16

    if snake:
        pos = chip // 2 + lax.rem(chip, 2) * (chips - 1 - 2 * (chip // 2))
    else:
        pos = chip

    def device_at(p, c):
        p = lax.rem(p + 2 * chips, chips)
        if snake:
            y = p // hops
            return 2 * (2 * (p + y * (chips - 1 - 2 * p)) + y) + c
        return 2 * p + c

    def eig_copy(g):
        slot = lax.rem(g, EIG_SLOTS)
        return pltpu.make_async_copy(
            eig_ref.at[:, pl.ds(pl.multiple_of(g * group_rows, group_rows), group_rows)],
            eigv.at[slot], eig_sem.at[slot])

    for g in range(EIG_SLOTS - 1):
        eig_copy(g).start()

    barrier = pltpu.get_barrier_semaphore()

    @pl.loop(1, n)
    def _(r):
        pl.semaphore_signal(barrier, inc=1, device_id={"docs": lax.rem(me + r, n)}, device_id_type=MESH)

    mine = dact_ref[0].astype(f32)
    for k in range(FOLDS):
        for b in range(fold // 128):
            at = k * fold + b * 128
            own[b, pl.ds(k, tokens, stride=FOLDS), :] = mine[:, at:at + 128]
    for b in range(fold // 128):
        buf[me, :, b * 128:(b + 1) * 128] = own[b].astype(bf16)

    def ring_copy(way, step, h):
        sign = 1 - 2 * way
        block = device_at(pos - sign * (step - 1), core)
        view = buf.at[block, :, pl.ds(pl.multiple_of(h * half, half), half)]
        return pltpu.make_async_remote_copy(
            src_ref=view, dst_ref=view,
            send_sem=ring_send.at[way, step - 1, h], recv_sem=ring_recv.at[way, step - 1, h],
            device_id={"docs": device_at(pos + sign, core)}, device_id_type=MESH)

    def ring_arrival(way, step, h):
        sign = 1 - 2 * way
        block = device_at(pos - sign * step, core)
        view = buf.at[block, :, pl.ds(pl.multiple_of(h * half, half), half)]
        return pltpu.make_async_remote_copy(
            src_ref=view, dst_ref=view,
            send_sem=ring_send.at[way, step - 1, h], recv_sem=ring_recv.at[way, step - 1, h],
            device_id={"docs": device_at(pos + sign, core)}, device_id_type=MESH)

    def cross_copy(p, c):
        p = lax.rem(p + 2 * chips, chips)
        view = buf.at[device_at(p, c)]
        return pltpu.make_async_remote_copy(
            src_ref=view, dst_ref=view,
            send_sem=cross_send.at[p], recv_sem=cross_recv.at[p],
            device_id={"docs": 2 * chip + 1 - core}, device_id_type=MESH)

    pl.semaphore_wait(barrier, n - 1)
    for h in range(2):
        for way in range(2):
            ring_copy(way, 1, h).start()
    cross_copy(pos, core).start()

    for q in range(queries):
        qgt[q] = qgrad_ref[q].astype(f32).T.astype(bf16)

    slot_of = lax.broadcasted_iota(jnp.int32, (tokens, dgrad_ref.shape[2]), 0)
    gown[...] = jnp.where(slot_of < len_ref[0], dgrad_ref[0].astype(f32), 0.0)
    gtmp[...] = jnp.zeros_like(gtmp)

    @pl.loop(0, n)
    def _(to):
        start = pl.multiple_of((to * slab) // 128 * 128, 128)
        for side in range(2):
            for b in range(2):
                at = pl.multiple_of(start + side * 256 + b * 128, 128)
                gtmp[b, pl.ds(side, tokens, stride=2), :] = gown[:, pl.ds(at, 128)]
        gsend[to] = jnp.concatenate([gtmp[0], gtmp[1]], axis=1).astype(bf16)

    grecv[me] = gsend[me]

    def g_copy(slot, to):
        return pltpu.make_async_remote_copy(
            src_ref=gsend.at[to], dst_ref=grecv.at[slot],
            send_sem=g_send.at[to], recv_sem=g_recv.at[slot],
            device_id={"docs": to}, device_id_type=MESH)

    def make_pre(g):
        slot = lax.rem(g, EIG_SLOTS)
        eig_copy(g).wait()

        @pl.when(g + EIG_SLOTS - 1 < groups)
        def _():
            eig_copy(g + EIG_SLOTS - 1).start()

        @pl.loop(0, group_rows // CHUNK)
        def _(c):
            local = pl.multiple_of(c * CHUNK, CHUNK)
            at = pl.multiple_of(g * group_rows + c * CHUNK, CHUNK)
            inv = 1.0 / (eigv[slot, :, pl.ds(local, CHUNK)].astype(f32) + damping)
            for q in range(queries):
                gram = jnp.dot(qgt[q], qact_ref[q, :, pl.ds(at, CHUNK)], preferred_element_type=f32)
                pre[q * slab:(q + 1) * slab, pl.ds(at, CHUNK)] = (gram * inv).astype(bf16)

    @pl.loop(0, chips - 2)
    def _(e):
        make_pre(e)
        step = e // 2 + 1
        h = lax.rem(e, 2)
        for way in range(2):
            ring_arrival(way, step, h).wait_recv()

            @pl.when(step + 1 < hops)
            def _():
                ring_copy(way, step + 1, h).start()

        @pl.when(e == chips - 4)
        def _():
            ring_copy(0, hops, 0).start()

        @pl.when(e == chips - 3)
        def _():
            ring_copy(1, hops, 1).start()

        @pl.when(h == 1)
        def _():
            cross_copy(pos - step, core).start()
            cross_copy(pos + step, core).start()

    @pl.loop(1, n)
    def _(r):
        g_copy(me, lax.rem(me + r, n)).start()

    make_pre(chips - 2)
    ring_arrival(0, hops, 0).wait_recv()
    ring_arrival(1, hops, 1).wait_recv()
    cross_copy(pos + hops, core).start()
    make_pre(chips - 1)

    @pl.loop(0, chips)
    def _(p):
        cross_copy(p, 1 - core).wait_recv()

    @pl.loop(0, n)
    def _(d):
        block = buf[d].astype(f32)
        for t in range(tokens):
            at = pl.ds(pl.multiple_of((t * n + d) * FOLDS, FOLDS), FOLDS)
            for b in range(fold // 128):
                wide[b, at, :] = block[t * FOLDS:(t + 1) * FOLDS, b * 128:(b + 1) * 128]


    acc[...] = jnp.zeros_like(acc)

    @pl.loop(0, FOLDS)
    def _(k):
        for b in range(fold // 128):
            actb[:, b * 128:(b + 1) * 128] = wide[b, pl.ds(k, tokens * n, stride=FOLDS), :].astype(bf16)
        acc[...] += lax.dot_general(
            pre[:, pl.ds(pl.multiple_of(k * fold, fold), fold)], actb[...],
            (((1,), (1,)), ((), ())), preferred_element_type=f32)

    @pl.loop(1, n)
    def _(r):
        g_copy(lax.rem(me + r, n), me).wait_recv()

    @pl.loop(0, n)
    def _(d):
        got = grecv[d].astype(f32)
        for b in range(2):
            gwide[b, pl.ds(pl.multiple_of(d * 16, 16), 16), :] = got[:, b * 128:(b + 1) * 128]

    part[...] = jnp.zeros_like(part)
    rows[...] = jnp.zeros_like(rows)
    grads[...] = jnp.zeros_like(grads)
    odd = lax.rem(me, 2) == 1
    for t in range(tokens):
        window = jnp.concatenate(
            [gwide[b, pl.ds(t * 2 + side, n, stride=16), :] for side in range(2) for b in range(2)], axis=1)
        moved = jnp.concatenate([window[:, 64:], window[:, :64]], axis=1)
        grads[t * n:(t + 1) * n, :] = jnp.where(odd, moved, window)
    gradt[...] = grads[...].T
    for q in range(queries):
        rows[q:q + 1, :tokens * n] = jnp.sum(
            acc[q * slab:(q + 1) * slab, :] * gradt[:slab, :tokens * n], axis=0, keepdims=True)
    scores = rows[...].T
    total = scores[0:n]
    for t in range(1, tokens):
        total += scores[t * n:(t + 1) * n]
    part[pl.ds(0, n, stride=8), :] = total

    def p_copy(slot, to):
        return pltpu.make_async_remote_copy(
            src_ref=part.at[pl.ds(pl.multiple_of(to * 8, 8), 8)],
            dst_ref=parts.at[pl.ds(pl.multiple_of(slot * 8, 8), 8)],
            send_sem=p_send.at[to], recv_sem=p_recv.at[slot],
            device_id={"docs": to}, device_id_type=MESH)

    @pl.loop(1, n)
    def _(r):
        p_copy(me, lax.rem(me + r, n)).start()

    mine_at = pl.ds(pl.multiple_of(me * 8, 8), 8)
    parts[mine_at, :] = part[mine_at, :]

    for h in range(2):
        for way in range(2):
            @pl.loop(1, hops)
            def _(s):
                ring_copy(way, s, h).wait_send()
    ring_copy(0, hops, 0).wait_send()
    ring_copy(1, hops, 1).wait_send()

    @pl.loop(0, chips)
    def _(p):
        cross_copy(p, core).wait_send()

    @pl.loop(1, n)
    def _(r):
        g_copy(me, lax.rem(me + r, n)).wait_send()

    @pl.loop(1, n)
    def _(r):
        p_copy(lax.rem(me + r, n), me).wait_recv()

    total = parts[0:8, :]
    for d in range(1, n):
        total += parts[d * 8:d * 8 + 8, :]
    out_ref[...] = total[0:1, :queries] * scale

    @pl.loop(1, n)
    def _(r):
        p_copy(me, lax.rem(me + r, n)).wait_send()


def body(query_act, query_grad, eigenvalues, doc_act, doc_grad, doc_len):
    queries, qtokens, width = query_act.shape
    tokens = doc_act.shape[1]
    slab = eigenvalues.shape[1]
    n = lax.axis_size("docs")
    chips = n // 2
    fold = width // FOLDS
    columns = queries * slab
    padded = -(-n * tokens // 128) * 128
    scale = 1.0 / (5.0 * math.sqrt(qtokens * width * slab * n * tokens))
    vmem = pl.BlockSpec(memory_space=pltpu.VMEM)
    dma = pltpu.SemaphoreType.DMA
    return pl.pallas_call(
        functools.partial(kernel, n, scale),
        out_shape=jax.ShapeDtypeStruct((1, queries), f32),
        in_specs=[pl.BlockSpec(memory_space=pltpu.SMEM), vmem, vmem, pl.BlockSpec(memory_space=pl.ANY), vmem, vmem],
        out_specs=vmem,
        scratch_shapes=[
            pltpu.VMEM((n, tokens * FOLDS, fold), bf16),
            pltpu.VMEM((fold // 128, n * tokens * FOLDS, 128), f32),
            pltpu.VMEM((n * tokens, fold), bf16),
            pltpu.VMEM((columns, width), bf16),
            pltpu.VMEM((EIG_SLOTS, slab, width // chips), bf16),
            pltpu.VMEM((queries, slab, qtokens), bf16),
            pltpu.VMEM((fold // 128, tokens * FOLDS, 128), f32),
            pltpu.VMEM((tokens, doc_grad.shape[2]), f32),
            pltpu.VMEM((2, 16, 128), f32),
            pltpu.VMEM((n, 16, 256), bf16),
            pltpu.VMEM((n, 16, 256), bf16),
            pltpu.VMEM((2, n * 16, 128), f32),
            pltpu.VMEM((padded, 512), f32),
            pltpu.VMEM((512, padded), f32),
            pltpu.VMEM((columns, n * tokens), f32),
            pltpu.VMEM((128, padded), f32),
            pltpu.VMEM((n * 8, 128), f32),
            pltpu.VMEM((n * 8, 128), f32),
            dma((EIG_SLOTS,)),
            dma((2, chips // 2, 2)),
            dma((2, chips // 2, 2)),
            dma((chips,)),
            dma((chips,)),
            dma((n,)),
            dma((n,)),
            dma((n,)),
            dma((n,)),
        ],
        compiler_params=pltpu.CompilerParams(
            collective_id=0, has_side_effects=True, vmem_limit_bytes=62 * 1024 * 1024),
    )(doc_len, query_act, query_grad, eigenvalues.T, doc_act, doc_grad).T


def solution(mesh):
    in_specs = (
        P("groups", None, None),
        P("groups", None, "docs"),
        P(None, "docs"),
        P(("groups", "docs"), None, None),
        P(("groups", "docs"), None, None),
        P(("groups", "docs")),
    )
    out_specs = P(None, ("groups", "docs"))
    return jax.shard_map(body, mesh=mesh, in_specs=in_specs, out_specs=out_specs, check_vma=False)
```
